32 devices in a mesh: lat: 4 (over y, core), lon: 8 (over z, x).
Axes of the slice: x: 2, y: 2, z: 4, core: 2. Of those that a mesh axis runs over, the one named last changes fastest.
Arguments:
- field: bfloat16 [64, 512, 256], P('lat', 'lon'), may hold values from -6 to 6
- filters: bfloat16 [64, 4, 9, 264], P('lat'), may hold values from -0.1875 to 0.1875
- sector_width: int32 [8], P('lat'), may hold values from 1 to 2, as said below
- block_offset: int32 [8, 4], P('lat'), may hold values from -8 to 7, as said below
- mixing: bfloat16 [9, 32, 256], replicated, may hold values from -0.375 to 0.375
Outputs:
- output: bfloat16 [64, 512, 256], P('lat', 'lon')
The draws below stay inside these ranges and needn't reach their ends.
Inputs may be any that keep to these rules, and one draw needn't show every extreme that they name: `sector_width`: the last row group has width 2, some row group has width 1. `block_offset`: in units of 8 longitudes; the last row group holds both ends of the range.
All inputs are finite; a program needn't handle non-finite values.
Results may differ from the reference program's by a relative error of at most 0.0049.
Values may be sent and summed in bfloat16 or wider, within the bound.
A program may use at most 128 MiB of HBM per device.

```python
import jax
import jax.numpy as jnp
from jax import lax

K = 9
C = 256
G = 8
R = 16
RG = 8
NB = 4
BW = 8
SMAX = 2
LON_DEV = 64
CG = 32
RSPAN = 33
NROWS = 64
NLON = 512


def draw_sector_width(key, part):
    key = jax.random.fold_in(key, 11)
    groups = NROWS // RG
    first_key = jax.random.fold_in(key, 1)
    second_key = jax.random.fold_in(key, 2)
    position = jnp.arange(groups, dtype=jnp.int32)
    values = jax.random.randint(first_key, (groups,), 1, SMAX + 1, dtype=jnp.int32)
    narrow = jax.random.randint(second_key, (), 0, groups - 1, dtype=jnp.int32)
    values = jnp.where(position == narrow, 1, values)
    values = jnp.where(position == groups - 1, SMAX, values)
    return values.astype(jnp.int32)


def draw_block_offset(key, part):
    key = jax.random.fold_in(key, 23)
    groups = NROWS // RG
    reach = LON_DEV // BW
    values = jax.random.randint(key, (groups, NB), -reach, reach, dtype=jnp.int32)
    values = values.at[groups - 1, 0].set(-reach)
    values = values.at[groups - 1, 1].set(reach - 1)
    return values.astype(jnp.int32)


def shard_levels(own_key, dims, cuts, least, high):
    factor_of = 1.0
    for dim, parts in cuts:
        draws = jax.random.uniform(jax.random.fold_in(jax.random.fold_in(own_key, 6), dim), (parts,), jnp.float32, least / len(cuts), high / len(cuts))
        factor_of = factor_of * jnp.repeat(jnp.exp(draws), dims[dim] // parts).reshape((-1,) + (1,) * (len(dims) - 1 - dim))
    return factor_of


def noise(key, shape, scale, most, split=(), held_as=jnp.bfloat16):
    factor_of = shard_levels(key, shape, split, -0.22, 0.18) if split else 1.0
    result = jax.random.normal(key, shape, jnp.float32) * scale * factor_of
    return jnp.minimum(jnp.maximum(result, -most), most).astype(held_as)


def setup_inputs(seed: int = 0) -> dict:
    key_of = jax.random.split(jax.random.key(seed), 6)
    return {
        "field": noise(key_of[0], (NROWS, NLON, C), 1.0, 6.0, ((0, 4), (1, 8))),
        "filters": noise(key_of[1], (NROWS, NB, K, RSPAN * BW), (RSPAN * NB * BW) ** -0.5, 0.1875, ((0, 4),)),
        "sector_width": draw_sector_width(jax.random.fold_in(key_of[5], 71), 0),
        "block_offset": draw_block_offset(jax.random.fold_in(key_of[5], 71), 0),
        "mixing": noise(key_of[4], (K, CG, C), (K * CG) ** -0.5, 0.375),
    }


def reference(field, filters, sector_width, block_offset, mixing):
    halo_lon = SMAX * LON_DEV
    padded = jnp.pad(field, ((R, R), (0, 0), (0, 0)))
    wrapped = jnp.concatenate([padded[:, NLON - halo_lon:], padded, padded[:, :halo_lon]], axis=1)
    shifts = (BW * block_offset * sector_width[:, None]).astype(jnp.int32)
    mix_table = mixing.astype(jnp.float32).reshape(K, CG, G, CG)

    def one_row(row_index):
        row_group = row_index // RG
        weights = filters[row_index].astype(jnp.float32).reshape(NB, K, 2 * R + 1, BW)
        response_sum = jnp.zeros((K, NLON, C), jnp.float32)
        for block_index in range(NB):
            start = (halo_lon + shifts[row_group, block_index]).astype(jnp.int32)
            window = lax.dynamic_slice(wrapped, (row_index.astype(jnp.int32), start, jnp.int32(0)), (2 * R + 1, NLON + BW - 1, C)).astype(jnp.float32)
            for column in range(BW):
                response_sum = response_sum + jnp.einsum('kr,rlc->klc', weights[block_index, :, :, column], window[:, column:column + NLON])
        rounded = lax.optimization_barrier(response_sum.astype(jnp.bfloat16))
        response = rounded.astype(jnp.float32).reshape(K, NLON, G, CG)
        mixed = jnp.einsum('klgc,kcgo->lgo', response, mix_table)
        return mixed.reshape(NLON, C).astype(jnp.bfloat16)

    return lax.map(one_row, jnp.arange(NROWS, dtype=jnp.int32))
```

```python
import jax
import jax.numpy as jnp
from jax import lax
from jax.experimental import pallas as pl
from jax.experimental.pallas import tpu as pltpu
from jax.sharding import PartitionSpec as P

K = 9
G = 8
R = 16
RG = 8
NB = 4
BW = 8
SMAX = 2
CG = 32
LANES = 128
WIDE = G * CG
PER = LANES // CG
TALL = RG + 2 * R
SLAB = TALL * BW
VMEM_LIMIT = 56 * 1024 * 1024


def swap_chunks(parts):
    rows = parts[0].shape[0]
    chunk = lax.broadcasted_iota(jnp.int32, (rows, LANES), 1) // CG
    outs = []
    for g in range(G):
        g1, g0 = divmod(g, PER)
        halves = []
        for m1 in range(G // PER):
            acc = None
            for m0 in range(PER):
                piece = parts[m1 * PER + m0][:, g1 * LANES : (g1 + 1) * LANES]
                turn = (CG * (m0 - g0)) % LANES
                if turn:
                    piece = pltpu.roll(piece, turn, 1)
                acc = piece if acc is None else jnp.where(chunk == m0, piece, acc)
            halves.append(acc)
        outs.append(jnp.concatenate(halves, axis=1))
    return outs


def pack_kernel(field_ref, out_ref):
    rows = field_ref.shape[0]
    value = field_ref[...].astype(jnp.float32).reshape(rows, G, BW, WIDE)
    parts = [value[:, m].reshape(rows * BW, WIDE) for m in range(G)]
    for g, block in enumerate(swap_chunks(parts)):
        out_ref[g] = block.astype(jnp.bfloat16)


def unpack_kernel(in_ref, out_ref):
    rows = out_ref.shape[0]
    parts = [in_ref[g].astype(jnp.float32) for g in range(G)]
    blocks = [b.reshape(rows, 1, BW, WIDE) for b in swap_chunks(parts)]
    whole = jnp.concatenate(blocks, axis=1).reshape(rows, G * BW, WIDE)
    out_ref[...] = whole.astype(jnp.bfloat16)


def toeplitz_kernel(spread_ref, out_ref):
    groups = spread_ref.shape[0]
    width = 2 * SLAB
    v = lax.broadcasted_iota(jnp.int32, (BW, width), 0)
    lane = lax.broadcasted_iota(jnp.int32, (BW, width), 1)
    u = lane % BW
    score = jnp.where(lane < SLAB, u - v, v - u - 1)
    keep = score >= 0
    keep_first = jnp.where(lane // BW == TALL - 1, -1, score) >= 0
    keep_last = jnp.where(lane // BW == TALL, -1, score) >= 0

    def body(index, carry):
        group, k = index // K, index % K
        rows = spread_ref[group, k]
        blocks = []
        for p in range(RG):
            kept = {0: keep_first, RG - 1: keep_last}.get(p, keep)
            pieces = []
            for b in range(NB):
                row = rows[p : p + 1, b * width : (b + 1) * width]
                wide = jnp.broadcast_to(row, (BW, width))
                turned = pltpu.roll(wide, 0, 1, stride=1, stride_axis=0)
                pieces.append(jnp.where(kept, turned, 0.0))
            blocks.append(jnp.concatenate(pieces, axis=1))
        tall = jnp.concatenate(blocks, axis=0).astype(jnp.bfloat16)
        out_ref[group, pl.ds(pl.multiple_of(k * RG * BW, RG * BW), RG * BW), :] = tall
        return carry

    lax.fori_loop(0, groups * K, body, 0)


def main_kernel(shift_ref, ext_ref, weights_ref, mix_ref, out_ref, turned, side, response):
    sectors = ext_ref.shape[0]
    rows = ext_ref.shape[1]
    groups = weights_ref.shape[0]
    lane = lax.broadcasted_iota(jnp.int32, (rows, LANES), 1)

    def turn(sector, carry):
        after = jnp.minimum(sector + 1, sectors - 1)
        first = ext_ref[sector][:, :LANES].astype(jnp.float32)
        second = ext_ref[sector][:, LANES:].astype(jnp.float32)
        third = ext_ref[after][:, :LANES].astype(jnp.float32)
        turned[0, 2 * sector] = ext_ref[sector][:, :LANES]
        turned[0, 2 * sector + 1] = ext_ref[sector][:, LANES:]
        for r in range(1, PER):
            back = LANES - CG * r
            x, y, z = [pltpu.roll(t, back, 1) for t in (first, second, third)]
            turned[r, 2 * sector] = jnp.where(lane < back, x, y).astype(jnp.bfloat16)
            turned[r, 2 * sector + 1] = jnp.where(lane < back, y, z).astype(jnp.bfloat16)
        return carry

    lax.fori_loop(0, sectors, turn, 0)

    for group in range(groups):

        def tile(s, carry):
            for b in range(NB):
                for half in range(2):
                    shift = shift_ref[group, b] + (half + SMAX * BW)
                    r, step = shift % PER, shift // PER
                    low = (b * 2 + half) * SLAB
                    for j in range(2):
                        side[low : low + SLAB, j * LANES : (j + 1) * LANES] = turned[
                            r, 2 * s + j + step, group * RG * BW : group * RG * BW + SLAB, :
                        ]
            sums = jnp.dot(weights_ref[group], side[...], preferred_element_type=jnp.float32)
            rounded = sums.astype(jnp.bfloat16)
            for k in range(K):
                response[k, s] = rounded[k * RG * BW : (k + 1) * RG * BW]
            return carry

        lax.fori_loop(0, G, tile, 0)
        mixed = jnp.zeros((G * RG * BW, WIDE), jnp.float32)
        for k in range(K):
            left = response[k].reshape(G * RG * BW, WIDE)
            mixed = mixed + jnp.dot(left, mix_ref[k], preferred_element_type=jnp.float32)
        out_ref[:, group * RG * BW : (group + 1) * RG * BW, :] = mixed.astype(jnp.bfloat16).reshape(
            G, RG * BW, WIDE
        )


def spread_filters(filters):
    rows = filters.shape[0]
    groups = rows // RG
    taps = filters.shape[3]
    f = filters.reshape(groups, RG, NB, K, taps).transpose(0, 3, 1, 2, 4)
    placed = []
    for p in range(RG):
        one = f[:, :, p]
        low = jnp.pad(one, ((0, 0), (0, 0), (0, 0), (BW * p, 2 * SLAB - BW * p - taps)))
        start = SLAB - BW + BW * p
        high = jnp.pad(one, ((0, 0), (0, 0), (0, 0), (start, 2 * SLAB - start - taps)))
        placed.append(low + high)
    whole = jnp.stack(placed, axis=2)
    return whole.reshape(groups, K, RG, NB * 2 * SLAB).astype(jnp.float32)


def call(kernel, shape, *args, scratch=(), specs=None):
    return pl.pallas_call(
        kernel,
        out_shape=jax.ShapeDtypeStruct(shape, jnp.bfloat16),
        in_specs=specs or [pl.BlockSpec(memory_space=pltpu.VMEM)] * len(args),
        out_specs=pl.BlockSpec(memory_space=pltpu.VMEM),
        scratch_shapes=list(scratch),
        compiler_params=pltpu.CompilerParams(vmem_limit_bytes=VMEM_LIMIT),
    )(*args)


def on_device(field, filters, sector_width, block_offset, mixing):
    rows, lon_dev, chans = field.shape
    groups = rows // RG
    lons = lax.axis_size("lon")
    lats = lax.axis_size("lat")
    segments = lons // G
    cuts = None
    if segments > 1:
        cuts = [[s * G + i for i in range(G)] for s in range(segments)]
    channel_group = lax.axis_index("lon") % G

    packed = call(pack_kernel, (G, rows * BW, WIDE), field)
    own = lax.all_to_all(packed, "lon", 0, 0, axis_index_groups=cuts, tiled=True)
    up = [(i, i + 1) for i in range(lats - 1)]
    down = [(i + 1, i) for i in range(lats - 1)]
    above = lax.ppermute(own, "lat", up)
    below = lax.ppermute(own, "lat", down)
    tall = jnp.concatenate([above, own, below], axis=1)
    if segments > 1:
        forward = [(i, (i + G) % lons) for i in range(lons)]
        back = [(j, i) for i, j in forward]
        west = lax.ppermute(tall[G - SMAX :], "lon", forward)
        east = lax.ppermute(tall[:SMAX], "lon", back)
    else:
        west, east = tall[G - SMAX :], tall[:SMAX]
    ext = jnp.concatenate([west, tall, east], axis=0)

    weights = call(toeplitz_kernel, (groups, K * RG * BW, NB * 2 * SLAB), spread_filters(filters))
    own_mix = lax.dynamic_slice_in_dim(mixing, channel_group * CG, CG, 2)
    eye = (jnp.arange(WIDE)[:, None] // CG) == (jnp.arange(WIDE)[None, :] // CG)
    big_mix = jnp.where(eye[None], jnp.tile(own_mix, (1, G, G)), jnp.zeros((), mixing.dtype))
    shifts = block_offset * sector_width[:, None]

    vmem = pl.BlockSpec(memory_space=pltpu.VMEM)
    mixed = call(
        main_kernel,
        (G, rows * BW, WIDE),
        shifts,
        ext,
        weights,
        big_mix,
        scratch=[
            pltpu.VMEM((PER, 2 * (G + 2 * SMAX), (rows + 2 * R) * BW, LANES), jnp.bfloat16),
            pltpu.VMEM((NB * 2 * SLAB, WIDE), jnp.bfloat16),
            pltpu.VMEM((K, G, RG * BW, WIDE), jnp.bfloat16),
        ],
        specs=[pl.BlockSpec(memory_space=pltpu.SMEM), vmem, vmem, vmem],
    )
    home = lax.all_to_all(mixed, "lon", 0, 0, axis_index_groups=cuts, tiled=True)
    return call(unpack_kernel, (rows, lon_dev, chans), home)


def solution(mesh):
    return jax.shard_map(
        on_device,
        mesh=mesh,
        in_specs=(P("lat", "lon", None), P("lat", None, None, None), P("lat"), P("lat", None), P()),
        out_specs=P("lat", "lon", None),
        check_vma=False,
    )
```

```python
import functools

import jax
import jax.numpy as jnp
from jax import lax
from jax.experimental import pallas as pl
from jax.experimental.pallas import tpu as pltpu
from jax.sharding import PartitionSpec as P

K = 9
G = 8
R = 16
RG = 8
NB = 4
BW = 8
SMAX = 2
CG = 32
LANES = 128
WIDE = G * CG
PER = LANES // CG
TALL = RG + 2 * R
SLAB = TALL * BW
VMEM_LIMIT = 56 * 1024 * 1024


def swap_chunks(parts):
    rows = parts[0].shape[0]
    chunk = lax.broadcasted_iota(jnp.int32, (rows, LANES), 1) // CG
    outs = []
    for g in range(G):
        g1, g0 = divmod(g, PER)
        halves = []
        for m1 in range(G // PER):
            acc = None
            for m0 in range(PER):
                piece = parts[m1 * PER + m0][:, g1 * LANES : (g1 + 1) * LANES]
                turn = (CG * (m0 - g0)) % LANES
                if turn:
                    piece = pltpu.roll(piece, turn, 1)
                acc = piece if acc is None else jnp.where(chunk == m0, piece, acc)
            halves.append(acc)
        outs.append(jnp.concatenate(halves, axis=1))
    return outs


def peers(steps):
    me = lax.axis_index("lon") % G
    base = lax.axis_index("lon") - me
    other = (me + steps) % G
    return other, (lax.axis_index("lat"), base + other)


def lay_filters(spread_ref, out_ref, first, last):
    width = 2 * SLAB
    v = lax.broadcasted_iota(jnp.int32, (BW, width), 0)
    lane = lax.broadcasted_iota(jnp.int32, (BW, width), 1)
    u = lane % BW
    keep_low = jnp.where(lane < SLAB, u - v, -1) >= 0
    keep_high = jnp.where(lane < SLAB, -1, v - u - 1) >= 0

    def body(index, carry):
        group, k = index // K, index % K
        rows = spread_ref[group, k]
        blocks = []
        for p in range(RG):
            pieces = []
            for b in range(NB):
                row = rows[p : p + 1, b * width : (b + 1) * width]
                wide = jnp.broadcast_to(row, (BW, width))
                low = pltpu.roll(wide, BW * p, 1, stride=1, stride_axis=0)
                high = pltpu.roll(wide, SLAB - BW + BW * p, 1, stride=1, stride_axis=0)
                pieces.append(jnp.where(keep_low, low, jnp.where(keep_high, high, 0.0)))
            blocks.append(jnp.concatenate(pieces, axis=1))
        tall = jnp.concatenate(blocks, axis=0).astype(jnp.bfloat16)
        out_ref[group, pl.ds(pl.multiple_of(k * RG * BW, RG * BW), RG * BW), :] = tall
        return carry

    lax.fori_loop(first, last, body, 0)


def exchange_kernel(lats, field_ref, spread_ref, tall_ref, weights_ref, packed, sent, got, halo_sent, halo_got):
    rows = field_ref.shape[0]
    size = rows * BW
    lat, lon = lax.axis_index("lat"), lax.axis_index("lon")
    me, _ = peers(0)
    has_up, has_down = lat > 0, lat < lats - 1
    barrier = pltpu.get_barrier_semaphore()
    for d in range(1, G):
        pl.semaphore_signal(barrier, inc=1, device_id=peers(d)[1], device_id_type=pl.DeviceIdType.MESH)

    @pl.when(has_up)
    def _():
        pl.semaphore_signal(barrier, inc=1, device_id=(lat - 1, lon), device_id_type=pl.DeviceIdType.MESH)

    @pl.when(has_down)
    def _():
        pl.semaphore_signal(barrier, inc=1, device_id=(lat + 1, lon), device_id_type=pl.DeviceIdType.MESH)

    value = field_ref[...].astype(jnp.float32).reshape(rows, G, BW, WIDE)
    parts = [value[:, m].reshape(size, WIDE) for m in range(G)]
    for g, block in enumerate(swap_chunks(parts)):
        packed[g] = block.astype(jnp.bfloat16)

    count = G - 1 + jnp.where(has_up, 1, 0) + jnp.where(has_down, 1, 0)
    pl.semaphore_wait(barrier, count)

    def swap(d):
        other, device = peers(d)
        return pltpu.make_async_remote_copy(
            src_ref=packed.at[other],
            dst_ref=tall_ref.at[me, pl.ds(size, size)],
            send_sem=sent.at[d],
            recv_sem=got.at[d],
            device_id=device,
            device_id_type=pl.DeviceIdType.MESH,
        )

    def halo(d, side):
        sector, _ = peers(G - d)
        return pltpu.make_async_remote_copy(
            src_ref=tall_ref.at[sector, pl.ds(size, size)],
            dst_ref=tall_ref.at[sector, pl.ds(0 if side else 2 * size, size)],
            send_sem=halo_sent.at[side, d],
            recv_sem=halo_got.at[side, d],
            device_id=(lat + 1 if side else lat - 1, lon),
            device_id_type=pl.DeviceIdType.MESH,
        )

    order = [1, 7, 2, 6, 3, 5, 4]
    for d in order:
        swap(d).start()
    tall_ref[me, size : 2 * size] = packed[me]

    def forward(d):
        @pl.when(has_up)
        def _():
            halo(d, 0).start()

        @pl.when(has_down)
        def _():
            halo(d, 1).start()

    forward(0)
    steps = spread_ref.shape[0] * K
    lay_filters(spread_ref, weights_ref, 0, steps // 2)
    for d in order:
        swap(d).wait_recv()
        forward(d)
    lay_filters(spread_ref, weights_ref, steps // 2, steps)

    blank = jnp.zeros((G, size, WIDE), jnp.bfloat16)

    @pl.when(lat == 0)
    def _():
        tall_ref[:, 0:size] = blank

    @pl.when(lat == lats - 1)
    def _():
        tall_ref[:, 2 * size : 3 * size] = blank

    for d in order:
        swap(d).wait_send()
    for d in range(G):

        @pl.when(has_up)
        def _():
            halo(d, 0).wait_send()
            halo(d, 1).wait_recv()

        @pl.when(has_down)
        def _():
            halo(d, 1).wait_send()
            halo(d, 0).wait_recv()


def home_kernel(in_ref, out_ref, held, sent, got):
    rows = out_ref.shape[0]
    me, _ = peers(0)
    barrier = pltpu.get_barrier_semaphore()
    for d in range(1, G):
        pl.semaphore_signal(barrier, inc=1, device_id=peers(d)[1], device_id_type=pl.DeviceIdType.MESH)
    pl.semaphore_wait(barrier, G - 1)

    def swap(d):
        other, device = peers(d)
        return pltpu.make_async_remote_copy(
            src_ref=in_ref.at[other],
            dst_ref=held.at[me],
            send_sem=sent.at[d],
            recv_sem=got.at[d],
            device_id=device,
            device_id_type=pl.DeviceIdType.MESH,
        )

    for d in range(1, G):
        swap(d).start()
    held[me] = in_ref[me]
    for d in range(1, G):
        swap(d).wait_recv()
    parts = [held[g].astype(jnp.float32) for g in range(G)]
    blocks = [b.reshape(rows, 1, BW, WIDE) for b in swap_chunks(parts)]
    whole = jnp.concatenate(blocks, axis=1).reshape(rows, G * BW, WIDE)
    out_ref[...] = whole.astype(jnp.bfloat16)
    for d in range(1, G):
        swap(d).wait_send()


def make_mix(group, mixing_ref, big):
    lane = lax.broadcasted_iota(jnp.int32, (CG, WIDE), 1) // CG
    row_block = lax.broadcasted_iota(jnp.int32, (WIDE, WIDE), 0) // CG
    lane_block = lax.broadcasted_iota(jnp.int32, (WIDE, WIDE), 1) // CG
    for k in range(K):
        one = jnp.where(lane == group, mixing_ref[k].astype(jnp.float32), 0.0)
        for turn in (CG, 2 * CG, 4 * CG):
            one = one + pltpu.roll(one, turn, 1)
        tall = jnp.concatenate([one] * G, axis=0)
        big[k] = jnp.where(row_block == lane_block, tall, 0.0).astype(jnp.bfloat16)


def main_kernel(shift_ref, ext_ref, weights_ref, mixing_ref, out_ref, turned, side, response, mix_ref):
    sectors = ext_ref.shape[0]
    rows = ext_ref.shape[1]
    groups = weights_ref.shape[0]
    lane = lax.broadcasted_iota(jnp.int32, (rows, LANES), 1)
    make_mix(shift_ref[0, NB], mixing_ref, mix_ref)

    def turn(sector, carry):
        after = jnp.minimum(sector + 1, sectors - 1)
        first = ext_ref[sector][:, :LANES].astype(jnp.float32)
        second = ext_ref[sector][:, LANES:].astype(jnp.float32)
        third = ext_ref[after][:, :LANES].astype(jnp.float32)
        turned[0, 2 * sector] = ext_ref[sector][:, :LANES]
        turned[0, 2 * sector + 1] = ext_ref[sector][:, LANES:]
        for r in range(1, PER):
            back = LANES - CG * r
            x, y, z = [pltpu.roll(t, back, 1) for t in (first, second, third)]
            turned[r, 2 * sector] = jnp.where(lane < back, x, y).astype(jnp.bfloat16)
            turned[r, 2 * sector + 1] = jnp.where(lane < back, y, z).astype(jnp.bfloat16)
        return carry

    lax.fori_loop(0, sectors, turn, 0)

    for group in range(groups):

        def tile(s, carry):
            for b in range(NB):
                for half in range(2):
                    shift = shift_ref[group, b] + (half + SMAX * BW)
                    r, step = shift % PER, shift // PER
                    low = (b * 2 + half) * SLAB
                    for j in range(2):
                        side[low : low + SLAB, j * LANES : (j + 1) * LANES] = turned[
                            r, 2 * s + j + step, group * RG * BW : group * RG * BW + SLAB, :
                        ]
            sums = jnp.dot(weights_ref[group], side[...], preferred_element_type=jnp.float32)
            rounded = sums.astype(jnp.bfloat16)
            for k in range(K):
                response[k, s] = rounded[k * RG * BW : (k + 1) * RG * BW]
            return carry

        lax.fori_loop(0, G, tile, 0)
        mixed = jnp.zeros((G * RG * BW, WIDE), jnp.float32)
        for k in range(K):
            left = response[k].reshape(G * RG * BW, WIDE)
            mixed = mixed + jnp.dot(left, mix_ref[k], preferred_element_type=jnp.float32)
        out_ref[:, group * RG * BW : (group + 1) * RG * BW, :] = mixed.astype(jnp.bfloat16).reshape(
            G, RG * BW, WIDE
        )


def spread_filters(filters):
    rows = filters.shape[0]
    groups = rows // RG
    taps = filters.shape[3]
    f = filters.reshape(groups, RG, NB, K, taps).transpose(0, 3, 1, 2, 4)
    f = jnp.pad(f.astype(jnp.float32), ((0, 0),) * 4 + ((0, 2 * SLAB - taps),))
    return f.reshape(groups, K, RG, NB * 2 * SLAB)


def call(kernel, shapes, *args, scratch=(), specs=None, ident=None):
    vmem = pl.BlockSpec(memory_space=pltpu.VMEM)
    return pl.pallas_call(
        kernel,
        out_shape=[jax.ShapeDtypeStruct(shape, jnp.bfloat16) for shape in shapes],
        in_specs=specs or [vmem] * len(args),
        out_specs=[vmem] * len(shapes),
        scratch_shapes=list(scratch),
        compiler_params=pltpu.CompilerParams(
            vmem_limit_bytes=VMEM_LIMIT, collective_id=ident, has_side_effects=ident is not None
        ),
    )(*args)


def on_device(field, filters, sector_width, block_offset, mixing):
    rows, lon_dev, chans = field.shape
    groups = rows // RG
    lons = lax.axis_size("lon")
    lats = lax.axis_size("lat")
    segments = lons // G
    size = rows * BW
    copies = pltpu.SemaphoreType.DMA((G,))
    halos = pltpu.SemaphoreType.DMA((2, G))

    tall, weights = call(
        functools.partial(exchange_kernel, lats),
        [(G, 3 * size, WIDE), (groups, K * RG * BW, NB * 2 * SLAB)],
        field,
        spread_filters(filters),
        scratch=[pltpu.VMEM((G, size, WIDE), jnp.bfloat16), copies, copies, halos, halos],
        ident=0,
    )
    if segments > 1:
        forward = [(i, (i + G) % lons) for i in range(lons)]
        back = [(j, i) for i, j in forward]
        west = lax.ppermute(tall[G - SMAX :], "lon", forward)
        east = lax.ppermute(tall[:SMAX], "lon", back)
    else:
        west, east = tall[G - SMAX :], tall[:SMAX]
    ext = jnp.concatenate([west, tall, east], axis=0)

    shifts = block_offset * sector_width[:, None]
    channel_group = jnp.broadcast_to(lax.axis_index("lon") % G, (groups, 1))
    scalars = jnp.concatenate([shifts, channel_group.astype(jnp.int32)], axis=1)

    vmem = pl.BlockSpec(memory_space=pltpu.VMEM)
    (mixed,) = call(
        main_kernel,
        [(G, size, WIDE)],
        scalars,
        ext,
        weights,
        mixing,
        scratch=[
            pltpu.VMEM((PER, 2 * (G + 2 * SMAX), (rows + 2 * R) * BW, LANES), jnp.bfloat16),
            pltpu.VMEM((NB * 2 * SLAB, WIDE), jnp.bfloat16),
            pltpu.VMEM((K, G, RG * BW, WIDE), jnp.bfloat16),
            pltpu.VMEM((K, WIDE, WIDE), jnp.bfloat16),
        ],
        specs=[pl.BlockSpec(memory_space=pltpu.SMEM), vmem, vmem, vmem],
    )
    (out,) = call(
        home_kernel,
        [(rows, lon_dev, chans)],
        mixed,
        scratch=[pltpu.VMEM((G, size, WIDE), jnp.bfloat16), copies, copies],
        ident=1,
    )
    return out


def solution(mesh):
    return jax.shard_map(
        on_device,
        mesh=mesh,
        in_specs=(P("lat", "lon", None), P("lat", None, None, None), P("lat"), P("lat", None), P()),
        out_specs=P("lat", "lon", None),
        check_vma=False,
    )
```

```python
import functools

import jax
import jax.numpy as jnp
from jax import lax
from jax.experimental import pallas as pl
from jax.experimental.pallas import tpu as pltpu
from jax.sharding import PartitionSpec as P

K = 9
G = 8
R = 16
RG = 8
NB = 4
BW = 8
SMAX = 2
CG = 32
LANES = 128
WIDE = G * CG
PER = LANES // CG
TALL = RG + 2 * R
SLAB = TALL * BW
VMEM_LIMIT = 56 * 1024 * 1024


def swap_chunks(parts):
    rows = parts[0].shape[0]
    chunk = lax.broadcasted_iota(jnp.int32, (rows, LANES), 1) // CG
    outs = []
    for g in range(G):
        g1, g0 = divmod(g, PER)
        halves = []
        for m1 in range(G // PER):
            acc = None
            for m0 in range(PER):
                piece = parts[m1 * PER + m0][:, g1 * LANES : (g1 + 1) * LANES]
                turn = (CG * (m0 - g0)) % LANES
                if turn:
                    piece = pltpu.roll(piece, turn, 1)
                acc = piece if acc is None else jnp.where(chunk == m0, piece, acc)
            halves.append(acc)
        outs.append(jnp.concatenate(halves, axis=1))
    return outs


def peers(steps):
    me = lax.axis_index("lon") % G
    base = lax.axis_index("lon") - me
    other = (me + steps) % G
    return other, (lax.axis_index("lat"), base + other)


def lay_filters(spread_ref, out_ref, first, last):
    width = 2 * SLAB
    v = lax.broadcasted_iota(jnp.int32, (BW, width), 0)
    lane = lax.broadcasted_iota(jnp.int32, (BW, width), 1)
    u = lane % BW
    keep_low = jnp.where(lane < SLAB, u - v, -1) >= 0
    keep_high = jnp.where(lane < SLAB, -1, v - u - 1) >= 0

    def body(index, carry):
        group, k = index // K, index % K
        rows = spread_ref[group, k]
        blocks = []
        for p in range(RG):
            pieces = []
            for b in range(NB):
                row = rows[p : p + 1, b * width : (b + 1) * width]
                wide = jnp.broadcast_to(row, (BW, width))
                low = pltpu.roll(wide, BW * p, 1, stride=1, stride_axis=0)
                high = pltpu.roll(wide, SLAB - BW + BW * p, 1, stride=1, stride_axis=0)
                pieces.append(jnp.where(keep_low, low, jnp.where(keep_high, high, 0.0)))
            blocks.append(jnp.concatenate(pieces, axis=1))
        tall = jnp.concatenate(blocks, axis=0).astype(jnp.bfloat16)
        out_ref[group, pl.ds(pl.multiple_of(k * RG * BW, RG * BW), RG * BW), :] = tall
        return carry

    lax.fori_loop(first, last, body, 0)


def exchange_kernel(lats, field_ref, spread_ref, tall_ref, weights_ref, packed, sent, got, halo_sent, halo_got):
    rows = field_ref.shape[0]
    size = rows * BW
    lat, lon = lax.axis_index("lat"), lax.axis_index("lon")
    me, _ = peers(0)
    has_up, has_down = lat > 0, lat < lats - 1
    barrier = pltpu.get_barrier_semaphore()
    for d in range(1, G):
        pl.semaphore_signal(barrier, inc=1, device_id=peers(d)[1], device_id_type=pl.DeviceIdType.MESH)

    @pl.when(has_up)
    def _():
        pl.semaphore_signal(barrier, inc=1, device_id=(lat - 1, lon), device_id_type=pl.DeviceIdType.MESH)

    @pl.when(has_down)
    def _():
        pl.semaphore_signal(barrier, inc=1, device_id=(lat + 1, lon), device_id_type=pl.DeviceIdType.MESH)

    value = field_ref[...].astype(jnp.float32).reshape(rows, G, BW, WIDE)
    parts = [value[:, m].reshape(size, WIDE) for m in range(G)]
    for g, block in enumerate(swap_chunks(parts)):
        packed[g] = block.astype(jnp.bfloat16)

    count = G - 1 + jnp.where(has_up, 1, 0) + jnp.where(has_down, 1, 0)
    pl.semaphore_wait(barrier, count)

    def swap(d):
        other, device = peers(d)
        return pltpu.make_async_remote_copy(
            src_ref=packed.at[other],
            dst_ref=tall_ref.at[me, pl.ds(size, size)],
            send_sem=sent.at[d],
            recv_sem=got.at[d],
            device_id=device,
            device_id_type=pl.DeviceIdType.MESH,
        )

    def halo(d, side):
        sector, _ = peers(G - d)
        return pltpu.make_async_remote_copy(
            src_ref=tall_ref.at[sector, pl.ds(size, size)],
            dst_ref=tall_ref.at[sector, pl.ds(0 if side else 2 * size, size)],
            send_sem=halo_sent.at[side, d],
            recv_sem=halo_got.at[side, d],
            device_id=(lat + 1 if side else lat - 1, lon),
            device_id_type=pl.DeviceIdType.MESH,
        )

    order = [1, 7, 2, 6, 3, 5, 4]
    for d in order:
        swap(d).start()
    tall_ref[me, size : 2 * size] = packed[me]

    def forward(d):
        @pl.when(has_up)
        def _():
            halo(d, 0).start()

        @pl.when(has_down)
        def _():
            halo(d, 1).start()

    forward(0)
    steps = spread_ref.shape[0] * K
    lay_filters(spread_ref, weights_ref, 0, steps // 2)
    for d in order:
        swap(d).wait_recv()
        forward(d)
    lay_filters(spread_ref, weights_ref, steps // 2, steps)

    blank = jnp.zeros((G, size, WIDE), jnp.bfloat16)

    @pl.when(lat == 0)
    def _():
        tall_ref[:, 0:size] = blank

    @pl.when(lat == lats - 1)
    def _():
        tall_ref[:, 2 * size : 3 * size] = blank

    for d in order:
        swap(d).wait_send()
    for d in range(G):

        @pl.when(has_up)
        def _():
            halo(d, 0).wait_send()
            halo(d, 1).wait_recv()

        @pl.when(has_down)
        def _():
            halo(d, 1).wait_send()
            halo(d, 0).wait_recv()


def unpack_kernel(in_ref, out_ref):
    rows = out_ref.shape[0]
    parts = [in_ref[g].astype(jnp.float32) for g in range(G)]
    blocks = [b.reshape(rows, 1, BW, WIDE) for b in swap_chunks(parts)]
    whole = jnp.concatenate(blocks, axis=1).reshape(rows, G * BW, WIDE)
    out_ref[...] = whole.astype(jnp.bfloat16)


def make_mix(group, mixing_ref, big):
    lane = lax.broadcasted_iota(jnp.int32, (CG, WIDE), 1) // CG
    row_block = lax.broadcasted_iota(jnp.int32, (WIDE, WIDE), 0) // CG
    lane_block = lax.broadcasted_iota(jnp.int32, (WIDE, WIDE), 1) // CG
    for k in range(K):
        one = jnp.where(lane == group, mixing_ref[k].astype(jnp.float32), 0.0)
        for turn in (CG, 2 * CG, 4 * CG):
            one = one + pltpu.roll(one, turn, 1)
        tall = jnp.concatenate([one] * G, axis=0)
        big[k] = jnp.where(row_block == lane_block, tall, 0.0).astype(jnp.bfloat16)


def main_kernel(
    shift_ref, ext_ref, weights_ref, mixing_ref, out_ref, turned, side, response, mix_ref, mixed_ref, sent, got
):
    sectors, rows, _ = ext_ref.shape
    groups = weights_ref.shape[0]
    tiles = 2 * sectors
    closed = sectors == G
    size = RG * BW
    me, _ = peers(0)
    barrier = pltpu.get_barrier_semaphore()
    for d in range(1, G):
        pl.semaphore_signal(barrier, inc=1, device_id=peers(d)[1], device_id_type=pl.DeviceIdType.MESH)
    lane = lax.broadcasted_iota(jnp.int32, (rows, LANES), 1)
    make_mix(shift_ref[0, NB], mixing_ref, mix_ref)

    def turn(sector, carry):
        after = (sector + 1) % sectors
        first = ext_ref[sector][:, :LANES].astype(jnp.float32)
        second = ext_ref[sector][:, LANES:].astype(jnp.float32)
        third = ext_ref[after][:, :LANES].astype(jnp.float32)
        turned[0, 2 * sector] = ext_ref[sector][:, :LANES]
        turned[0, 2 * sector + 1] = ext_ref[sector][:, LANES:]
        for r in range(1, PER):
            back = LANES - CG * r
            x, y, z = [pltpu.roll(t, back, 1) for t in (first, second, third)]
            turned[r, 2 * sector] = jnp.where(lane < back, x, y).astype(jnp.bfloat16)
            turned[r, 2 * sector + 1] = jnp.where(lane < back, y, z).astype(jnp.bfloat16)
        return carry

    lax.fori_loop(0, sectors, turn, 0)

    def swap(group, d):
        other, device = peers(d)
        part = pl.ds(group * size, size)
        return pltpu.make_async_remote_copy(
            src_ref=mixed_ref.at[other, part],
            dst_ref=out_ref.at[me, part],
            send_sem=sent.at[group, d],
            recv_sem=got.at[group, d],
            device_id=device,
            device_id_type=pl.DeviceIdType.MESH,
        )

    for group in range(groups):

        def fill(slot, s):
            for b in range(NB):
                for half in range(2):
                    shift = shift_ref[group, b] + (half + SMAX * BW)
                    r, step = shift % PER, shift // PER
                    low = (b * 2 + half) * SLAB
                    for j in range(2):
                        index = 2 * s + j + step
                        if closed:
                            index = (index + tiles - 2 * SMAX) % tiles
                        side[slot, low : low + SLAB, j * LANES : (j + 1) * LANES] = turned[
                            r, index, group * size : group * size + SLAB, :
                        ]

        def multiply(slot, s):
            sums = jnp.dot(weights_ref[group], side[slot], preferred_element_type=jnp.float32)
            rounded = sums.astype(jnp.bfloat16)
            for k in range(K):
                response[k, s] = rounded[k * size : (k + 1) * size]

        def pair(i, carry):
            fill(1, 2 * i + 1)
            multiply(0, 2 * i)
            fill(0, jnp.minimum(2 * i + 2, G - 1))
            multiply(1, 2 * i + 1)
            return carry

        fill(0, 0)
        lax.fori_loop(0, G // 2, pair, 0)
        mixed = jnp.zeros((G * size, WIDE), jnp.float32)
        for k in range(K):
            left = response[k].reshape(G * size, WIDE)
            mixed = mixed + jnp.dot(left, mix_ref[k], preferred_element_type=jnp.float32)
        part = slice(group * size, (group + 1) * size)
        mixed_ref[:, part, :] = mixed.astype(jnp.bfloat16).reshape(G, size, WIDE)
        if group == 0:
            pl.semaphore_wait(barrier, G - 1)
        for d in range(1, G):
            swap(group, d).start()
        out_ref[me, part, :] = mixed_ref[me, part, :]

    for group in range(groups):
        for d in range(1, G):
            swap(group, d).wait()


def spread_filters(filters):
    rows = filters.shape[0]
    groups = rows // RG
    taps = filters.shape[3]
    f = filters.reshape(groups, RG, NB, K, taps).transpose(0, 3, 1, 2, 4)
    f = jnp.pad(f.astype(jnp.float32), ((0, 0),) * 4 + ((0, 2 * SLAB - taps),))
    return f.reshape(groups, K, RG, NB * 2 * SLAB)


def call(kernel, shapes, *args, scratch=(), specs=None, ident=None):
    vmem = pl.BlockSpec(memory_space=pltpu.VMEM)
    return pl.pallas_call(
        kernel,
        out_shape=[jax.ShapeDtypeStruct(shape, jnp.bfloat16) for shape in shapes],
        in_specs=specs or [vmem] * len(args),
        out_specs=[vmem] * len(shapes),
        scratch_shapes=list(scratch),
        compiler_params=pltpu.CompilerParams(
            vmem_limit_bytes=VMEM_LIMIT, collective_id=ident, has_side_effects=ident is not None
        ),
    )(*args)


def on_device(field, filters, sector_width, block_offset, mixing):
    rows, lon_dev, chans = field.shape
    groups = rows // RG
    lons = lax.axis_size("lon")
    lats = lax.axis_size("lat")
    segments = lons // G
    size = rows * BW
    copies = pltpu.SemaphoreType.DMA((G,))
    halos = pltpu.SemaphoreType.DMA((2, G))

    tall, weights = call(
        functools.partial(exchange_kernel, lats),
        [(G, 3 * size, WIDE), (groups, K * RG * BW, NB * 2 * SLAB)],
        field,
        spread_filters(filters),
        scratch=[pltpu.VMEM((G, size, WIDE), jnp.bfloat16), copies, copies, halos, halos],
        ident=0,
    )
    if segments > 1:
        forward = [(i, (i + G) % lons) for i in range(lons)]
        back = [(j, i) for i, j in forward]
        west = lax.ppermute(tall[G - SMAX :], "lon", forward)
        east = lax.ppermute(tall[:SMAX], "lon", back)
        ext = jnp.concatenate([west, tall, east], axis=0)
    else:
        ext = tall

    shifts = block_offset * sector_width[:, None]
    channel_group = jnp.broadcast_to(lax.axis_index("lon") % G, (groups, 1))
    scalars = jnp.concatenate([shifts, channel_group.astype(jnp.int32)], axis=1)

    vmem = pl.BlockSpec(memory_space=pltpu.VMEM)
    (mixed,) = call(
        main_kernel,
        [(G, size, WIDE)],
        scalars,
        ext,
        weights,
        mixing,
        scratch=[
            pltpu.VMEM((PER, 2 * ext.shape[0], (rows + 2 * R) * BW, LANES), jnp.bfloat16),
            pltpu.VMEM((2, NB * 2 * SLAB, WIDE), jnp.bfloat16),
            pltpu.VMEM((K, G, RG * BW, WIDE), jnp.bfloat16),
            pltpu.VMEM((K, WIDE, WIDE), jnp.bfloat16),
            pltpu.VMEM((G, size, WIDE), jnp.bfloat16),
            pltpu.SemaphoreType.DMA((groups, G)),
            pltpu.SemaphoreType.DMA((groups, G)),
        ],
        specs=[pl.BlockSpec(memory_space=pltpu.SMEM), vmem, vmem, vmem],
        ident=1,
    )
    (out,) = call(unpack_kernel, [(rows, lon_dev, chans)], mixed)
    return out


def solution(mesh):
    return jax.shard_map(
        on_device,
        mesh=mesh,
        in_specs=(P("lat", "lon", None), P("lat", None, None, None), P("lat"), P("lat", None), P()),
        out_specs=P("lat", "lon", None),
        check_vma=False,
    )
```

```python
import functools

import jax
import jax.numpy as jnp
from jax import lax
from jax.experimental import pallas as pl
from jax.experimental.pallas import tpu as pltpu
from jax.sharding import PartitionSpec as P

K = 9
G = 8
R = 16
RG = 8
NB = 4
BW = 8
SMAX = 2
CG = 32
LANES = 128
WIDE = G * CG
PER = LANES // CG
TALL = RG + 2 * R
SLAB = TALL * BW
VMEM_LIMIT = 56 * 1024 * 1024


def swap_chunks(parts):
    rows = parts[0].shape[0]
    chunk = lax.broadcasted_iota(jnp.int32, (rows, LANES), 1) // CG
    outs = []
    for g in range(G):
        g1, g0 = divmod(g, PER)
        halves = []
        for m1 in range(G // PER):
            acc = None
            for m0 in range(PER):
                piece = parts[m1 * PER + m0][:, g1 * LANES : (g1 + 1) * LANES]
                turn = (CG * (m0 - g0)) % LANES
                if turn:
                    piece = pltpu.roll(piece, turn, 1)
                acc = piece if acc is None else jnp.where(chunk == m0, piece, acc)
            halves.append(acc)
        outs.append(jnp.concatenate(halves, axis=1))
    return outs


def peers(steps):
    me = lax.axis_index("lon") % G
    base = lax.axis_index("lon") - me
    other = (me + steps) % G
    return other, (lax.axis_index("lat"), base + other)


def lay_filters(spread_ref, out_ref, first, last):
    width = 2 * SLAB
    v = lax.broadcasted_iota(jnp.int32, (BW, width), 0)
    lane = lax.broadcasted_iota(jnp.int32, (BW, width), 1)
    u = lane % BW
    score = jnp.where(lane < SLAB, u - v, v - u - 1)
    keep = score >= 0
    keep_first = jnp.where(lane // BW == TALL - 1, -1, score) >= 0
    keep_last = jnp.where(lane // BW == TALL, -1, score) >= 0

    def body(index, carry):
        group, k = index // K, index % K
        rows = spread_ref[group, k]
        placed = []
        for b in range(NB):
            taps = rows[:, b * width : (b + 1) * width]
            low = pltpu.roll(taps, 0, 1, stride=BW, stride_axis=0)
            high = pltpu.roll(taps, SLAB - BW, 1, stride=BW, stride_axis=0)
            placed.append(low + high)
        blocks = []
        for p in range(RG):
            kept = {0: keep_first, RG - 1: keep_last}.get(p, keep)
            pieces = []
            for b in range(NB):
                wide = jnp.broadcast_to(placed[b][p : p + 1], (BW, width))
                turned = pltpu.roll(wide, 0, 1, stride=1, stride_axis=0)
                pieces.append(jnp.where(kept, turned, 0.0))
            blocks.append(jnp.concatenate(pieces, axis=1))
        tall = jnp.concatenate(blocks, axis=0).astype(jnp.bfloat16)
        out_ref[group, pl.ds(pl.multiple_of(k * RG * BW, RG * BW), RG * BW), :] = tall
        return carry

    lax.fori_loop(first, last, body, 0)


def exchange_kernel(lats, field_ref, spread_ref, tall_ref, weights_ref, packed, sent, got, halo_sent, halo_got):
    rows = field_ref.shape[0]
    size = rows * BW
    lat, lon = lax.axis_index("lat"), lax.axis_index("lon")
    me, _ = peers(0)
    has_up, has_down = lat > 0, lat < lats - 1
    barrier = pltpu.get_barrier_semaphore()
    for d in range(1, G):
        pl.semaphore_signal(barrier, inc=1, device_id=peers(d)[1], device_id_type=pl.DeviceIdType.MESH)

    @pl.when(has_up)
    def _():
        pl.semaphore_signal(barrier, inc=1, device_id=(lat - 1, lon), device_id_type=pl.DeviceIdType.MESH)

    @pl.when(has_down)
    def _():
        pl.semaphore_signal(barrier, inc=1, device_id=(lat + 1, lon), device_id_type=pl.DeviceIdType.MESH)

    value = field_ref[...].astype(jnp.float32).reshape(rows, G, BW, WIDE)
    parts = [value[:, m].reshape(size, WIDE) for m in range(G)]
    for g, block in enumerate(swap_chunks(parts)):
        packed[g] = block.astype(jnp.bfloat16)

    count = G - 1 + jnp.where(has_up, 1, 0) + jnp.where(has_down, 1, 0)
    pl.semaphore_wait(barrier, count)

    def swap(d):
        other, device = peers(d)
        return pltpu.make_async_remote_copy(
            src_ref=packed.at[other],
            dst_ref=tall_ref.at[me, pl.ds(size, size)],
            send_sem=sent.at[d],
            recv_sem=got.at[d],
            device_id=device,
            device_id_type=pl.DeviceIdType.MESH,
        )

    def halo(d, side):
        sector, _ = peers(G - d)
        return pltpu.make_async_remote_copy(
            src_ref=tall_ref.at[sector, pl.ds(size, size)],
            dst_ref=tall_ref.at[sector, pl.ds(0 if side else 2 * size, size)],
            send_sem=halo_sent.at[side, d],
            recv_sem=halo_got.at[side, d],
            device_id=(lat + 1 if side else lat - 1, lon),
            device_id_type=pl.DeviceIdType.MESH,
        )

    order = [1, 7, 2, 6, 3, 5, 4]
    for d in order:
        swap(d).start()
    tall_ref[me, size : 2 * size] = packed[me]

    def forward(d):
        @pl.when(has_up)
        def _():
            halo(d, 0).start()

        @pl.when(has_down)
        def _():
            halo(d, 1).start()

    forward(0)
    steps = spread_ref.shape[0] * K
    lay_filters(spread_ref, weights_ref, 0, steps // 2)
    for d in order:
        swap(d).wait_recv()
        forward(d)
    lay_filters(spread_ref, weights_ref, steps // 2, steps)

    blank = jnp.zeros((G, size, WIDE), jnp.bfloat16)

    @pl.when(lat == 0)
    def _():
        tall_ref[:, 0:size] = blank

    @pl.when(lat == lats - 1)
    def _():
        tall_ref[:, 2 * size : 3 * size] = blank

    for d in order:
        swap(d).wait_send()
    for d in range(G):

        @pl.when(has_up)
        def _():
            halo(d, 0).wait_send()
            halo(d, 1).wait_recv()

        @pl.when(has_down)
        def _():
            halo(d, 1).wait_send()
            halo(d, 0).wait_recv()


def unpack_kernel(in_ref, out_ref):
    rows = out_ref.shape[0]
    parts = [in_ref[g].astype(jnp.float32) for g in range(G)]
    blocks = [b.reshape(rows, 1, BW, WIDE) for b in swap_chunks(parts)]
    whole = jnp.concatenate(blocks, axis=1).reshape(rows, G * BW, WIDE)
    out_ref[...] = whole.astype(jnp.bfloat16)


def make_mix(group, mixing_ref, big):
    lane = lax.broadcasted_iota(jnp.int32, (CG, WIDE), 1) // CG
    row_block = lax.broadcasted_iota(jnp.int32, (WIDE, WIDE), 0) // CG
    lane_block = lax.broadcasted_iota(jnp.int32, (WIDE, WIDE), 1) // CG
    for k in range(K):
        one = jnp.where(lane == group, mixing_ref[k].astype(jnp.float32), 0.0)
        for turn in (CG, 2 * CG, 4 * CG):
            one = one + pltpu.roll(one, turn, 1)
        tall = jnp.concatenate([one] * G, axis=0)
        big[k] = jnp.where(row_block == lane_block, tall, 0.0).astype(jnp.bfloat16)


def main_kernel(
    shift_ref, ext_ref, weights_ref, mixing_ref, out_ref, turned, side, response, mix_ref, mixed_ref, sent, got
):
    sectors, rows, _ = ext_ref.shape
    groups = weights_ref.shape[0]
    tiles = 2 * sectors
    closed = sectors == G
    size = RG * BW
    me, _ = peers(0)
    barrier = pltpu.get_barrier_semaphore()
    for d in range(1, G):
        pl.semaphore_signal(barrier, inc=1, device_id=peers(d)[1], device_id_type=pl.DeviceIdType.MESH)
    lane = lax.broadcasted_iota(jnp.int32, (rows, LANES), 1)
    make_mix(shift_ref[0, NB], mixing_ref, mix_ref)

    def turn(sector, carry):
        after = (sector + 1) % sectors
        first = ext_ref[sector][:, :LANES].astype(jnp.float32)
        second = ext_ref[sector][:, LANES:].astype(jnp.float32)
        third = ext_ref[after][:, :LANES].astype(jnp.float32)
        turned[0, 2 * sector] = ext_ref[sector][:, :LANES]
        turned[0, 2 * sector + 1] = ext_ref[sector][:, LANES:]
        for r in range(1, PER):
            back = LANES - CG * r
            x, y, z = [pltpu.roll(t, back, 1) for t in (first, second, third)]
            turned[r, 2 * sector] = jnp.where(lane < back, x, y).astype(jnp.bfloat16)
            turned[r, 2 * sector + 1] = jnp.where(lane < back, y, z).astype(jnp.bfloat16)
        return carry

    lax.fori_loop(0, sectors, turn, 0)

    def swap(group, d):
        other, device = peers(d)
        part = pl.ds(group * size, size)
        return pltpu.make_async_remote_copy(
            src_ref=mixed_ref.at[other, part],
            dst_ref=out_ref.at[me, part],
            send_sem=sent.at[group, d],
            recv_sem=got.at[group, d],
            device_id=device,
            device_id_type=pl.DeviceIdType.MESH,
        )

    for group in range(groups):

        def fill(slot, s):
            for b in range(NB):
                for half in range(2):
                    shift = shift_ref[group, b] + (half + SMAX * BW)
                    r, step = shift % PER, shift // PER
                    low = (b * 2 + half) * SLAB
                    for j in range(2):
                        index = 2 * s + j + step
                        if closed:
                            index = (index + tiles - 2 * SMAX) % tiles
                        side[slot, low : low + SLAB, j * LANES : (j + 1) * LANES] = turned[
                            r, index, group * size : group * size + SLAB, :
                        ]

        def multiply(slot, s):
            sums = jnp.dot(weights_ref[group], side[slot], preferred_element_type=jnp.float32)
            rounded = sums.astype(jnp.bfloat16)
            for k in range(K):
                response[k, s] = rounded[k * size : (k + 1) * size]

        def pair(i, carry):
            fill(1, 2 * i + 1)
            multiply(0, 2 * i)
            fill(0, jnp.minimum(2 * i + 2, G - 1))
            multiply(1, 2 * i + 1)
            return carry

        fill(0, 0)
        lax.fori_loop(0, G // 2, pair, 0)
        mixed = jnp.zeros((G * size, WIDE), jnp.float32)
        for k in range(K):
            left = response[k].reshape(G * size, WIDE)
            mixed = mixed + jnp.dot(left, mix_ref[k], preferred_element_type=jnp.float32)
        part = slice(group * size, (group + 1) * size)
        mixed_ref[:, part, :] = mixed.astype(jnp.bfloat16).reshape(G, size, WIDE)
        if group == 0:
            pl.semaphore_wait(barrier, G - 1)
        for d in range(1, G):
            swap(group, d).start()
        out_ref[me, part, :] = mixed_ref[me, part, :]

    for group in range(groups):
        for d in range(1, G):
            swap(group, d).wait()


def spread_filters(filters):
    rows = filters.shape[0]
    groups = rows // RG
    taps = filters.shape[3]
    f = filters.reshape(groups, RG, NB, K, taps).transpose(0, 3, 1, 2, 4)
    f = jnp.pad(f.astype(jnp.float32), ((0, 0),) * 4 + ((0, 2 * SLAB - taps),))
    return f.reshape(groups, K, RG, NB * 2 * SLAB)


def call(kernel, shapes, *args, scratch=(), specs=None, ident=None):
    vmem = pl.BlockSpec(memory_space=pltpu.VMEM)
    return pl.pallas_call(
        kernel,
        out_shape=[jax.ShapeDtypeStruct(shape, jnp.bfloat16) for shape in shapes],
        in_specs=specs or [vmem] * len(args),
        out_specs=[vmem] * len(shapes),
        scratch_shapes=list(scratch),
        compiler_params=pltpu.CompilerParams(
            vmem_limit_bytes=VMEM_LIMIT, collective_id=ident, has_side_effects=ident is not None
        ),
    )(*args)


def on_device(field, filters, sector_width, block_offset, mixing):
    rows, lon_dev, chans = field.shape
    groups = rows // RG
    lons = lax.axis_size("lon")
    lats = lax.axis_size("lat")
    segments = lons // G
    size = rows * BW
    copies = pltpu.SemaphoreType.DMA((G,))
    halos = pltpu.SemaphoreType.DMA((2, G))

    tall, weights = call(
        functools.partial(exchange_kernel, lats),
        [(G, 3 * size, WIDE), (groups, K * RG * BW, NB * 2 * SLAB)],
        field,
        spread_filters(filters),
        scratch=[pltpu.VMEM((G, size, WIDE), jnp.bfloat16), copies, copies, halos, halos],
        ident=0,
    )
    if segments > 1:
        forward = [(i, (i + G) % lons) for i in range(lons)]
        back = [(j, i) for i, j in forward]
        west = lax.ppermute(tall[G - SMAX :], "lon", forward)
        east = lax.ppermute(tall[:SMAX], "lon", back)
        ext = jnp.concatenate([west, tall, east], axis=0)
    else:
        ext = tall

    shifts = block_offset * sector_width[:, None]
    channel_group = jnp.broadcast_to(lax.axis_index("lon") % G, (groups, 1))
    scalars = jnp.concatenate([shifts, channel_group.astype(jnp.int32)], axis=1)

    vmem = pl.BlockSpec(memory_space=pltpu.VMEM)
    (mixed,) = call(
        main_kernel,
        [(G, size, WIDE)],
        scalars,
        ext,
        weights,
        mixing,
        scratch=[
            pltpu.VMEM((PER, 2 * ext.shape[0], (rows + 2 * R) * BW, LANES), jnp.bfloat16),
            pltpu.VMEM((2, NB * 2 * SLAB, WIDE), jnp.bfloat16),
            pltpu.VMEM((K, G, RG * BW, WIDE), jnp.bfloat16),
            pltpu.VMEM((K, WIDE, WIDE), jnp.bfloat16),
            pltpu.VMEM((G, size, WIDE), jnp.bfloat16),
            pltpu.SemaphoreType.DMA((groups, G)),
            pltpu.SemaphoreType.DMA((groups, G)),
        ],
        specs=[pl.BlockSpec(memory_space=pltpu.SMEM), vmem, vmem, vmem],
        ident=1,
    )
    (out,) = call(unpack_kernel, [(rows, lon_dev, chans)], mixed)
    return out


def solution(mesh):
    return jax.shard_map(
        on_device,
        mesh=mesh,
        in_specs=(P("lat", "lon", None), P("lat", None, None, None), P("lat"), P("lat", None), P()),
        out_specs=P("lat", "lon", None),
        check_vma=False,
    )
```

```python
import functools

import jax
import jax.numpy as jnp
from jax import lax
from jax.experimental import pallas as pl
from jax.experimental.pallas import tpu as pltpu
from jax.sharding import PartitionSpec as P

K = 9
G = 8
R = 16
RG = 8
NB = 4
BW = 8
SMAX = 2
CG = 32
LANES = 128
WIDE = G * CG
PER = LANES // CG
TALL = RG + 2 * R
SLAB = TALL * BW
VMEM_LIMIT = 56 * 1024 * 1024


def swap_chunks(parts):
    rows = parts[0].shape[0]
    chunk = lax.broadcasted_iota(jnp.int32, (rows, LANES), 1) // CG
    outs = []
    for g in range(G):
        g1, g0 = divmod(g, PER)
        halves = []
        for m1 in range(G // PER):
            acc = None
            for m0 in range(PER):
                piece = parts[m1 * PER + m0][:, g1 * LANES : (g1 + 1) * LANES]
                turn = (CG * (m0 - g0)) % LANES
                if turn:
                    piece = pltpu.roll(piece, turn, 1)
                acc = piece if acc is None else jnp.where(chunk == m0, piece, acc)
            halves.append(acc)
        outs.append(jnp.concatenate(halves, axis=1))
    return outs


def peers(steps):
    me = lax.axis_index("lon") % G
    base = lax.axis_index("lon") - me
    other = (me + steps) % G
    return other, (lax.axis_index("lat"), base + other)


def lay_filters(spread_ref, out_ref, first, last):
    width = 2 * SLAB
    v = lax.broadcasted_iota(jnp.int32, (BW, width), 0)
    lane = lax.broadcasted_iota(jnp.int32, (BW, width), 1)
    u = lane % BW
    keep_low = jnp.where(lane < SLAB, u - v, -1) >= 0
    keep_high = jnp.where(lane < SLAB, -1, v - u - 1) >= 0

    def body(index, carry):
        group, k = index // K, index % K
        rows = spread_ref[group, k].astype(jnp.float32)
        blocks = []
        for p in range(RG):
            pieces = []
            for b in range(NB):
                row = rows[p : p + 1, b * width : (b + 1) * width]
                wide = jnp.broadcast_to(row, (BW, width))
                low = pltpu.roll(wide, BW * p, 1, stride=1, stride_axis=0)
                high = pltpu.roll(wide, SLAB - BW + BW * p, 1, stride=1, stride_axis=0)
                pieces.append(jnp.where(keep_low, low, jnp.where(keep_high, high, 0.0)))
            blocks.append(jnp.concatenate(pieces, axis=1))
        tall = jnp.concatenate(blocks, axis=0).astype(jnp.bfloat16)
        out_ref[group, pl.ds(pl.multiple_of(k * RG * BW, RG * BW), RG * BW), :] = tall
        return carry

    lax.fori_loop(first, last, body, 0)


def exchange_kernel(lats, field_ref, spread_ref, tall_ref, weights_ref, packed, sent, got, halo_sent, halo_got):
    rows = field_ref.shape[0]
    size = rows * BW
    lat, lon = lax.axis_index("lat"), lax.axis_index("lon")
    me, _ = peers(0)
    has_up, has_down = lat > 0, lat < lats - 1
    barrier = pltpu.get_barrier_semaphore()
    for d in range(1, G):
        pl.semaphore_signal(barrier, inc=1, device_id=peers(d)[1], device_id_type=pl.DeviceIdType.MESH)

    @pl.when(has_up)
    def _():
        pl.semaphore_signal(barrier, inc=1, device_id=(lat - 1, lon), device_id_type=pl.DeviceIdType.MESH)

    @pl.when(has_down)
    def _():
        pl.semaphore_signal(barrier, inc=1, device_id=(lat + 1, lon), device_id_type=pl.DeviceIdType.MESH)

    value = field_ref[...].astype(jnp.float32).reshape(rows, G, BW, WIDE)
    parts = [value[:, m].reshape(size, WIDE) for m in range(G)]
    for g, block in enumerate(swap_chunks(parts)):
        packed[g] = block.astype(jnp.bfloat16)

    count = G - 1 + jnp.where(has_up, 1, 0) + jnp.where(has_down, 1, 0)
    pl.semaphore_wait(barrier, count)

    def swap(d):
        other, device = peers(d)
        return pltpu.make_async_remote_copy(
            src_ref=packed.at[other],
            dst_ref=tall_ref.at[me, pl.ds(size, size)],
            send_sem=sent.at[d],
            recv_sem=got.at[d],
            device_id=device,
            device_id_type=pl.DeviceIdType.MESH,
        )

    def halo(d, side):
        sector, _ = peers(G - d)
        return pltpu.make_async_remote_copy(
            src_ref=tall_ref.at[sector, pl.ds(size, size)],
            dst_ref=tall_ref.at[sector, pl.ds(0 if side else 2 * size, size)],
            send_sem=halo_sent.at[side, d],
            recv_sem=halo_got.at[side, d],
            device_id=(lat + 1 if side else lat - 1, lon),
            device_id_type=pl.DeviceIdType.MESH,
        )

    order = [1, 7, 2, 6, 3, 5, 4]
    for d in order:
        swap(d).start()
    tall_ref[me, size : 2 * size] = packed[me]

    def forward(d):
        @pl.when(has_up)
        def _():
            halo(d, 0).start()

        @pl.when(has_down)
        def _():
            halo(d, 1).start()

    forward(0)
    steps = spread_ref.shape[0] * K
    lay_filters(spread_ref, weights_ref, 0, steps // 2)
    for d in order:
        swap(d).wait_recv()
        forward(d)
    lay_filters(spread_ref, weights_ref, steps // 2, steps)

    blank = jnp.zeros((G, size, WIDE), jnp.bfloat16)

    @pl.when(lat == 0)
    def _():
        tall_ref[:, 0:size] = blank

    @pl.when(lat == lats - 1)
    def _():
        tall_ref[:, 2 * size : 3 * size] = blank

    for d in order:
        swap(d).wait_send()
    for d in range(G):

        @pl.when(has_up)
        def _():
            halo(d, 0).wait_send()
            halo(d, 1).wait_recv()

        @pl.when(has_down)
        def _():
            halo(d, 1).wait_send()
            halo(d, 0).wait_recv()


def unpack_kernel(in_ref, out_ref):
    rows = out_ref.shape[0]
    parts = [in_ref[g].astype(jnp.float32) for g in range(G)]
    blocks = [b.reshape(rows, 1, BW, WIDE) for b in swap_chunks(parts)]
    whole = jnp.concatenate(blocks, axis=1).reshape(rows, G * BW, WIDE)
    out_ref[...] = whole.astype(jnp.bfloat16)


def make_mix(group, mixing_ref, big):
    lane = lax.broadcasted_iota(jnp.int32, (CG, WIDE), 1) // CG
    row_block = lax.broadcasted_iota(jnp.int32, (WIDE, WIDE), 0) // CG
    lane_block = lax.broadcasted_iota(jnp.int32, (WIDE, WIDE), 1) // CG
    for k in range(K):
        one = jnp.where(lane == group, mixing_ref[k].astype(jnp.float32), 0.0)
        for turn in (CG, 2 * CG, 4 * CG):
            one = one + pltpu.roll(one, turn, 1)
        tall = jnp.concatenate([one] * G, axis=0)
        big[k] = jnp.where(row_block == lane_block, tall, 0.0).astype(jnp.bfloat16)


def main_kernel(
    shift_ref, ext_ref, weights_ref, mixing_ref, out_ref, turned, side, response, mix_ref, mixed_ref, sent, got
):
    sectors, rows, _ = ext_ref.shape
    groups = weights_ref.shape[0]
    tiles = 2 * sectors
    closed = sectors == G
    size = RG * BW
    me, _ = peers(0)
    barrier = pltpu.get_barrier_semaphore()
    for d in range(1, G):
        pl.semaphore_signal(barrier, inc=1, device_id=peers(d)[1], device_id_type=pl.DeviceIdType.MESH)
    lane = lax.broadcasted_iota(jnp.int32, (rows, LANES), 1)
    make_mix(shift_ref[0, NB], mixing_ref, mix_ref)

    def turn(sector, carry):
        after = (sector + 1) % sectors
        first = ext_ref[sector][:, :LANES].astype(jnp.float32)
        second = ext_ref[sector][:, LANES:].astype(jnp.float32)
        third = ext_ref[after][:, :LANES].astype(jnp.float32)
        turned[0, 2 * sector] = ext_ref[sector][:, :LANES]
        turned[0, 2 * sector + 1] = ext_ref[sector][:, LANES:]
        for r in range(1, PER):
            back = LANES - CG * r
            x, y, z = [pltpu.roll(t, back, 1) for t in (first, second, third)]
            turned[r, 2 * sector] = jnp.where(lane < back, x, y).astype(jnp.bfloat16)
            turned[r, 2 * sector + 1] = jnp.where(lane < back, y, z).astype(jnp.bfloat16)
        return carry

    lax.fori_loop(0, sectors, turn, 0)

    def swap(group, d):
        other, device = peers(d)
        part = pl.ds(group * size, size)
        return pltpu.make_async_remote_copy(
            src_ref=mixed_ref.at[other, part],
            dst_ref=out_ref.at[me, part],
            send_sem=sent.at[group, d],
            recv_sem=got.at[group, d],
            device_id=device,
            device_id_type=pl.DeviceIdType.MESH,
        )

    for group in range(groups):

        def fill(slot, s):
            for b in range(NB):
                for half in range(2):
                    shift = shift_ref[group, b] + (half + SMAX * BW)
                    r, step = shift % PER, shift // PER
                    low = (b * 2 + half) * SLAB
                    for j in range(2):
                        index = 2 * s + j + step
                        if closed:
                            index = (index + tiles - 2 * SMAX) % tiles
                        side[slot, low : low + SLAB, j * LANES : (j + 1) * LANES] = turned[
                            r, index, group * size : group * size + SLAB, :
                        ]

        def multiply(slot, s):
            sums = jnp.dot(weights_ref[group], side[slot], preferred_element_type=jnp.float32)
            rounded = sums.astype(jnp.bfloat16)
            for k in range(K):
                response[k, s] = rounded[k * size : (k + 1) * size]

        def pair(i, carry):
            fill(1, 2 * i + 1)
            multiply(0, 2 * i)
            fill(0, jnp.minimum(2 * i + 2, G - 1))
            multiply(1, 2 * i + 1)
            return carry

        fill(0, 0)
        lax.fori_loop(0, G // 2, pair, 0)
        mixed = jnp.zeros((G * size, WIDE), jnp.float32)
        for k in range(K):
            left = response[k].reshape(G * size, WIDE)
            mixed = mixed + jnp.dot(left, mix_ref[k], preferred_element_type=jnp.float32)
        part = slice(group * size, (group + 1) * size)
        mixed_ref[:, part, :] = mixed.astype(jnp.bfloat16).reshape(G, size, WIDE)
        if group == 0:
            pl.semaphore_wait(barrier, G - 1)
        for d in range(1, G):
            swap(group, d).start()
        out_ref[me, part, :] = mixed_ref[me, part, :]

    for group in range(groups):
        for d in range(1, G):
            swap(group, d).wait()


def spread_filters(filters):
    rows = filters.shape[0]
    groups = rows // RG
    taps = filters.shape[3]
    f = filters.reshape(groups, RG, NB, K, taps).transpose(0, 3, 1, 2, 4)
    f = jnp.pad(f, ((0, 0),) * 4 + ((0, 2 * SLAB - taps),))
    return f.reshape(groups, K, RG, NB * 2 * SLAB)


def call(kernel, shapes, *args, scratch=(), specs=None, ident=None):
    vmem = pl.BlockSpec(memory_space=pltpu.VMEM)
    return pl.pallas_call(
        kernel,
        out_shape=[jax.ShapeDtypeStruct(shape, jnp.bfloat16) for shape in shapes],
        in_specs=specs or [vmem] * len(args),
        out_specs=[vmem] * len(shapes),
        scratch_shapes=list(scratch),
        compiler_params=pltpu.CompilerParams(
            vmem_limit_bytes=VMEM_LIMIT, collective_id=ident, has_side_effects=ident is not None
        ),
    )(*args)


def on_device(field, filters, sector_width, block_offset, mixing):
    rows, lon_dev, chans = field.shape
    groups = rows // RG
    lons = lax.axis_size("lon")
    lats = lax.axis_size("lat")
    segments = lons // G
    size = rows * BW
    copies = pltpu.SemaphoreType.DMA((G,))
    halos = pltpu.SemaphoreType.DMA((2, G))

    tall, weights = call(
        functools.partial(exchange_kernel, lats),
        [(G, 3 * size, WIDE), (groups, K * RG * BW, NB * 2 * SLAB)],
        field,
        spread_filters(filters),
        scratch=[pltpu.VMEM((G, size, WIDE), jnp.bfloat16), copies, copies, halos, halos],
        ident=0,
    )
    if segments > 1:
        forward = [(i, (i + G) % lons) for i in range(lons)]
        back = [(j, i) for i, j in forward]
        west = lax.ppermute(tall[G - SMAX :], "lon", forward)
        east = lax.ppermute(tall[:SMAX], "lon", back)
        ext = jnp.concatenate([west, tall, east], axis=0)
    else:
        ext = tall

    shifts = block_offset * sector_width[:, None]
    channel_group = jnp.broadcast_to(lax.axis_index("lon") % G, (groups, 1))
    scalars = jnp.concatenate([shifts, channel_group.astype(jnp.int32)], axis=1)

    vmem = pl.BlockSpec(memory_space=pltpu.VMEM)
    (mixed,) = call(
        main_kernel,
        [(G, size, WIDE)],
        scalars,
        ext,
        weights,
        mixing,
        scratch=[
            pltpu.VMEM((PER, 2 * ext.shape[0], (rows + 2 * R) * BW, LANES), jnp.bfloat16),
            pltpu.VMEM((2, NB * 2 * SLAB, WIDE), jnp.bfloat16),
            pltpu.VMEM((K, G, RG * BW, WIDE), jnp.bfloat16),
            pltpu.VMEM((K, WIDE, WIDE), jnp.bfloat16),
            pltpu.VMEM((G, size, WIDE), jnp.bfloat16),
            pltpu.SemaphoreType.DMA((groups, G)),
            pltpu.SemaphoreType.DMA((groups, G)),
        ],
        specs=[pl.BlockSpec(memory_space=pltpu.SMEM), vmem, vmem, vmem],
        ident=1,
    )
    (out,) = call(unpack_kernel, [(rows, lon_dev, chans)], mixed)
    return out


def solution(mesh):
    return jax.shard_map(
        on_device,
        mesh=mesh,
        in_specs=(P("lat", "lon", None), P("lat", None, None, None), P("lat"), P("lat", None), P()),
        out_specs=P("lat", "lon", None),
        check_vma=False,
    )
```
